256 devices in a mesh: grp: 4 (over y_lo, core), blk: 64 (over z, y_hi, x).
Axes of the slice: x: 4, y: 4 (y_hi: 2, y_lo: 2; y = y_hi * 2 + y_lo), z: 8, core: 2. Of those that a mesh axis runs over, the one named last changes fastest.
Arguments:
- images: bfloat16 [131072, 1152], P(('grp', 'blk')), may hold values from -6 to 6
- texts: bfloat16 [131072, 1152], P(('grp', 'blk')), may hold values from -6 to 6
- logit_scale: float32 [1], replicated, may hold values from 30 to 120
- logit_bias: float32 [1], replicated, may hold values from -4 to 0
Outputs:
- image_grad: bfloat16 [131072, 1152], P(('grp', 'blk'))
- text_grad: bfloat16 [131072, 1152], P(('grp', 'blk'))
The draws below stay inside these ranges and needn't reach their ends.
All inputs are finite; a program needn't handle non-finite values.
Results may differ from the reference program's by a relative error of at most 0.0081.
Values may be sent and summed in bfloat16 or wider, within the bound.
No kernel may reach another device: no remote copies, remote signals or barrier semaphores. Data moves between devices by JAX's collectives and lax.ppermute only.
A program may use at most 64 MiB of HBM per device.

```python
import math
import jax
import jax.numpy as jnp
from jax import lax

D = 1152
ROWS = 512
BATCH = 131072
N_GRP = 4
N_BLK = 64


def levels(rng, shape, cuts, smallest, top_value):
    def one(dim, shards_of):
        steps = jax.random.uniform(jax.random.fold_in(jax.random.fold_in(rng, 6), dim), (shards_of,), jnp.float32, smallest / len(cuts), top_value / len(cuts))
        return jnp.repeat(jnp.exp(steps), shape[dim] // shards_of).reshape((-1,) + (1,) * (len(shape) - dim - 1))

    level = one(*cuts[0])
    for cut in cuts[1:]:
        level = level * one(*cut)
    return level


def bell_draw(stream_key, dims, scale, bound, pieces=(), kind=jnp.bfloat16):
    loudness = levels(stream_key, dims, pieces, -0.22, 0.18) if pieces else 1.0
    values = jax.random.normal(stream_key, dims, jnp.float32) * scale * loudness
    return jnp.minimum(jnp.maximum(values, -bound), bound).astype(kind)


def setup_inputs(seed: int = 0) -> dict:
    splits = jax.random.split(jax.random.key(seed), 5)
    return {
        "images": bell_draw(splits[0], (BATCH, D), 1.0, 6.0, ((0, 256),)),
        "texts": bell_draw(splits[1], (BATCH, D), 1.0, 6.0, ((0, 256),)),
        "logit_scale": jnp.clip(jnp.exp(jax.random.uniform(splits[2], (1,), jnp.float32, math.log(30.0), math.log(120.0))), 30.0, 120.0),
        "logit_bias": jnp.clip(jax.random.uniform(splits[3], (1,), jnp.float32, -4.0, 0.0), -4.0, 0.0),
    }


def unit_rows(raw):
    values = raw.astype(jnp.float32)
    norm = jnp.sqrt(lax.optimization_barrier(jnp.sum(values * values, axis=-1, keepdims=True)) + 1e-06)
    return (values / norm, norm)

def partner(blocks):
    shaped = blocks.reshape((N_GRP // 2, 2) + blocks.shape[1:])
    return shaped[:, ::-1].reshape(blocks.shape)

def coefficients(left, right, scale, bias, own):
    logits = scale * jnp.einsum('gkrd,gksd->gkrs', left.astype(jnp.float32), right.astype(jnp.float32)) + bias
    if own:
        sign = 2.0 * jnp.eye(ROWS, dtype=jnp.float32) - 1.0
    else:
        sign = -jnp.ones((ROWS, ROWS), jnp.float32)
    return (scale * -sign * jax.nn.sigmoid(-sign * logits)).astype(jnp.bfloat16)

def reference(images, texts, logit_scale, logit_bias):
    scale = logit_scale[0]
    bias = logit_bias[0]
    image_unit, image_norm = unit_rows(images.reshape(N_GRP, N_BLK, ROWS, D))
    text_unit, text_norm = unit_rows(texts.reshape(N_GRP, N_BLK, ROWS, D))
    image_half = image_unit.astype(jnp.bfloat16)
    text_half = text_unit.astype(jnp.bfloat16)
    paired = [(text_half, True), (jnp.roll(text_half, 1, axis=1), False), (jnp.roll(text_half, 2, axis=1), False), (partner(text_half), False)]
    image_sum = jnp.zeros(image_unit.shape, jnp.float32)
    text_sum = jnp.zeros(text_unit.shape, jnp.float32)
    for number in range(4):
        other, own = paired[number]
        coef = coefficients(image_half, other, scale, bias, own)
        image_sum = image_sum + jnp.einsum('gkrs,gksd->gkrd', coef.astype(jnp.float32), other.astype(jnp.float32))
        term = jnp.einsum('gkrs,gkrd->gksd', coef.astype(jnp.float32), image_half.astype(jnp.float32))
        if number > 0:
            term = lax.optimization_barrier(term.astype(jnp.bfloat16)).astype(jnp.float32)
        if number == 1:
            term = jnp.roll(term, -1, axis=1)
        elif number == 2:
            term = jnp.roll(term, -2, axis=1)
        elif number == 3:
            term = partner(term)
        text_sum = text_sum + term
    image_grad = (image_sum - image_unit * lax.optimization_barrier(jnp.sum(image_unit * image_sum, axis=-1, keepdims=True))) / image_norm
    text_grad = (text_sum - text_unit * lax.optimization_barrier(jnp.sum(text_unit * text_sum, axis=-1, keepdims=True))) / text_norm
    return (image_grad.astype(jnp.bfloat16).reshape(BATCH, D), text_grad.astype(jnp.bfloat16).reshape(BATCH, D))
```

```python
import jax
import jax.numpy as jnp
from jax import lax
from jax.sharding import PartitionSpec as P

AXES = ("grp", "blk")
CUTS = (0, 256, 512)


def routes(groups, blocks):
    near, far, cross = [], [], []
    for g in range(groups):
        for k in range(blocks):
            me = g * blocks + k
            near.append((me, g * blocks + (k ^ 1)))
            other = (k + 1) % blocks if k % 2 else (k - 1) % blocks
            far.append((me, g * blocks + other))
            cross.append((me, (g ^ 1) * blocks + k))
    return near, far, cross


def unit_rows(raw):
    values = raw.astype(jnp.float32)
    norm = jnp.sqrt(jnp.sum(values * values, axis=-1, keepdims=True) + 1e-06)
    return (values / norm, norm)


def coefficients(left, right, scale, bias, own=False):
    logits = (
        scale
        * lax.dot_general(left, right, (((1,), (1,)), ((), ())), preferred_element_type=jnp.float32)
        + bias
    )
    if own:
        sign = 2.0 * jnp.eye(left.shape[0], dtype=jnp.float32) - 1.0
    else:
        sign = -jnp.ones(logits.shape, jnp.float32)
    return (scale * -sign * jax.nn.sigmoid(-sign * logits)).astype(jnp.bfloat16)


def product(coef, other):
    return jnp.dot(coef, other, preferred_element_type=jnp.float32)


def right_product(coef, rows):
    return lax.dot_general(coef, rows, (((0,), (0,)), ((), ())), preferred_element_type=jnp.float32)


def finish(total, unit, norm):
    return ((total - unit * jnp.sum(unit * total, axis=-1, keepdims=True)) / norm).astype(
        jnp.bfloat16
    )


def on_device(images, texts, logit_scale, logit_bias):
    scale = logit_scale[0]
    bias = logit_bias[0]
    near, far, cross = routes(lax.axis_size("grp"), lax.axis_size("blk"))
    even = lax.axis_index("blk") % 2 == 0
    first = jnp.where(even, texts, images)
    second = jnp.where(even, images, texts)
    first_unit, first_norm = unit_rows(first)
    second_unit, second_norm = unit_rows(second)
    first_half = first_unit.astype(jnp.bfloat16)
    second_half = second_unit.astype(jnp.bfloat16)

    spans = list(zip(CUTS, CUTS[1:]))
    near_in = [lax.ppermute(first_half[a:b], AXES, near) for a, b in spans]
    far_in = [lax.ppermute(second_half[a:b], AXES, far) for a, b in spans]
    near_next = [lax.ppermute(block, AXES, near) for block in far_in]
    far_next = [lax.ppermute(block, AXES, far) for block in near_in]
    first_cross = lax.ppermute(second_half, AXES, cross)
    second_cross = lax.ppermute(first_half, AXES, cross)

    own = coefficients(first_half, second_half, scale, bias, True)
    first_sum = product(own, second_half)
    second_sum = right_product(own, first_half)
    for block in [first_cross] + near_in + near_next:
        first_sum += product(coefficients(first_half, block, scale, bias), block)
    for block in [second_cross] + far_in + far_next:
        second_sum += product(coefficients(second_half, block, scale, bias), block)
    first_grad = finish(first_sum, first_unit, first_norm)
    second_grad = finish(second_sum, second_unit, second_norm)
    return (
        jnp.where(even, second_grad, first_grad),
        jnp.where(even, first_grad, second_grad),
    )


def solution(mesh):
    spec = P(AXES, None)
    return jax.shard_map(
        on_device,
        mesh=mesh,
        in_specs=(spec, spec, P(), P()),
        out_specs=(spec, spec),
        check_vma=False,
    )
```

```python
import functools

import jax
import jax.numpy as jnp
from jax import lax
from jax.experimental import pallas as pl
from jax.experimental.pallas import tpu as pltpu
from jax.sharding import PartitionSpec as P

AXES = ("grp", "blk")
VMEM = pl.BlockSpec(memory_space=pltpu.VMEM)
SMEM = pl.BlockSpec(memory_space=pltpu.SMEM)
HBM = pl.BlockSpec(memory_space=pltpu.HBM)
TILE = 128
MIB = 1024 * 1024


def routes(groups, blocks):
    near, far, cross = [], [], []
    for g in range(groups):
        for k in range(blocks):
            me = g * blocks + k
            near.append((me, g * blocks + (k ^ 1)))
            other = (k + 1) % blocks if k % 2 else (k - 1) % blocks
            far.append((me, g * blocks + other))
            cross.append((me, (g ^ 1) * blocks + k))
    return near, far, cross


def call(body, outs, in_specs, out_specs, scratch=(), aliases=None, limit=16):
    return pl.pallas_call(
        body,
        out_shape=outs,
        in_specs=in_specs,
        out_specs=out_specs,
        scratch_shapes=scratch,
        input_output_aliases=aliases or {},
        compiler_params=pltpu.CompilerParams(vmem_limit_bytes=limit * MIB),
        cost_estimate=pl.CostEstimate(flops=0, bytes_accessed=0, transcendentals=0),
    )


def shape(rows, width, dtype):
    return jax.ShapeDtypeStruct((rows, width), dtype)


def prepare_kernel(start, even, images, texts, *refs):
    *outs, both, sems = refs
    blocks = (outs[:3], outs[3:])
    rows = blocks[0][0].shape[0]
    tiles = rows // TILE

    def fetch(slot, source, tile):
        return pltpu.make_async_copy(
            source.at[pl.ds(start + tile * TILE, TILE)],
            blocks[slot][1].at[pl.ds(tile * TILE, TILE)],
            sems.at[slot, tile],
        )

    def begin(sources):
        for tile in range(tiles):
            for slot, source in enumerate(sources):
                fetch(slot, source, tile).start()

    @pl.when(even[0] == 1)
    def _():
        begin((texts, images))

    @pl.when(even[0] != 1)
    def _():
        begin((images, texts))

    for tile in range(tiles):
        at = pl.ds(tile * TILE, TILE)
        for slot, (half, raw, norm) in enumerate(blocks):
            fetch(slot, images, tile).wait()
            values = raw[at].astype(jnp.float32)
            size = jnp.sqrt(jnp.sum(values * values, axis=-1, keepdims=True) + 1e-06)
            inverse = 1.0 / size
            rounded = (values * inverse).astype(jnp.bfloat16)
            half[at] = rounded
            both[pl.ds(slot * rows + tile * TILE, TILE)] = rounded
            norm[at] = jnp.broadcast_to(inverse, (TILE, 128))


def prepare(start, rows, even, images, texts):
    width = images.shape[1]
    rounded = shape(rows, width, jnp.bfloat16)
    outs = [rounded, rounded, shape(rows, 128, jnp.float32)] * 2
    outs.append(shape(2 * rows, width, jnp.bfloat16))
    return call(
        functools.partial(prepare_kernel, start),
        outs,
        [SMEM, HBM, HBM],
        [VMEM] * len(outs),
        [pltpu.SemaphoreType.DMA((2, rows // TILE))],
        limit=50,
    )(even, images, texts)


def coefficients(scale, bias, left, right, diagonal=False):
    logits = scale * lax.dot_general(
        left, right, (((1,), (1,)), ((), ())), preferred_element_type=jnp.float32
    ) + bias
    if diagonal:
        here = lax.broadcasted_iota(jnp.int32, logits.shape, 0) == lax.broadcasted_iota(
            jnp.int32, logits.shape, 1
        )
        logits = jnp.where(here, -logits, logits)
        factor = jnp.where(here, -scale, scale)
    else:
        factor = scale
    return (factor / (1.0 + jnp.exp(-logits))).astype(jnp.bfloat16)


def product(coef, right):
    return jnp.dot(coef, right, preferred_element_type=jnp.float32)


def own_kernel(
    scalars, first1, first2, second1, second2,
    raw11, raw12, raw21, raw22, norm11, norm12, norm21, norm22,
    total1, total2, unit1, unit2, size1, size2,
):
    scale, bias = scalars[0], scalars[1]
    firsts, seconds = (first1, first2), (second1, second2)
    rows = first1.shape[0]
    for lefts, rights, total in ((firsts, seconds, total1), (seconds, firsts, total2)):
        for i, left in enumerate(lefts):
            at = pl.ds(i * rows, rows)
            for j, right in enumerate(rights):
                term = product(coefficients(scale, bias, left[...], right[...], i == j), right[...])
                total[at] = term if j == 0 else total[at] + term
    for raws, norms, unit, size in (
        ((raw11, raw12), (norm11, norm12), unit1, size1),
        ((raw21, raw22), (norm21, norm22), unit2, size2),
    ):
        for i in range(2):
            at = pl.ds(i * rows, rows)
            unit[at] = raws[i][...].astype(jnp.float32) * norms[i][:, :1]
            size[at] = norms[i][...]


def add_kernel(scalars, first1, first2, second1, second2, in1, in2, right1, right2, total1, total2):
    scale, bias = scalars[0], scalars[1]
    rows = first1.shape[0]
    for lefts, right, given, total in (
        ((first1, first2), right1, in1, total1),
        ((second1, second2), right2, in2, total2),
    ):
        for i, left in enumerate(lefts):
            at = pl.ds(i * rows, rows)
            total[at] = given[at] + product(coefficients(scale, bias, left[...], right[...]), right[...])


def cross_kernel(scalars, first1, first2, second1, second2, in1, in2, both, total1, total2):
    rows = first1.shape[0]
    add_kernel(
        scalars, first1, first2, second1, second2, in1, in2,
        both.at[pl.ds(rows, rows)], both.at[pl.ds(0, rows)], total1, total2,
    )


def last_kernel(
    slot, scalars, even, left1, left2, right, given, unit, norm, image_in, text_in,
    image_grad, text_grad, out, sems,
):
    del image_in, text_in
    scale, bias = scalars[0], scalars[1]
    rows = left1.shape[0]

    def give(tile, target):
        at = pl.ds(tile * TILE, TILE)
        return pltpu.make_async_copy(out.at[at], target.at[at], sems.at[tile])

    coefs = [coefficients(scale, bias, left[...], right[...]) for left in (left1, left2)]
    tiles = 2 * rows // TILE
    for tile in range(tiles):
        i, inner = divmod(tile * TILE, rows)
        at = pl.ds(tile * TILE, TILE)
        whole = given[at] + product(coefs[i][inner : inner + TILE], right[...])
        along = jnp.sum(unit[at] * whole, axis=-1, keepdims=True)
        out[at] = ((whole - unit[at] * along) * norm[at][:, :1]).astype(jnp.bfloat16)

        @pl.when((even[0] == 1) == (slot == 0))
        def _():
            give(tile, text_grad).start()

        @pl.when((even[0] == 1) != (slot == 0))
        def _():
            give(tile, image_grad).start()

    for tile in range(tiles):
        give(tile, text_grad).wait()


def first_last_kernel(scalars, even, left1, left2, right, given, unit, norm, *refs):
    last_kernel(0, scalars, even, left1, left2, right, given, unit, norm, None, None, *refs)


def on_device(images, texts, logit_scale, logit_bias):
    rows, width = images.shape
    near, far, cross = routes(lax.axis_size("grp"), lax.axis_size("blk"))
    even = (1 - lax.axis_index("blk") % 2).astype(jnp.int32).reshape(1)
    scalars = jnp.concatenate([logit_scale, logit_bias])

    half = rows // 2
    first1, raw11, norm11, second1, raw21, norm21, both1 = prepare(
        0, half, even, images, texts
    )
    first2, raw12, norm12, second2, raw22, norm22, both2 = prepare(
        half, half, even, images, texts
    )

    def send(block, route):
        return lax.ppermute(block, AXES, route)

    blocks = (first1, first2, second1, second2)
    totals = [shape(rows, width, jnp.float32)] * 2

    def add(body, total1, total2, *rights):
        return call(
            body, totals, [SMEM] + [VMEM] * (6 + len(rights)), [VMEM] * 2, aliases={5: 0, 6: 1}
        )(scalars, *blocks, total1, total2, *rights)

    far_a, near_a = send(second1, far), send(first1, near)
    far_b, near_b = send(second2, far), send(first2, near)
    cross1 = send(both1, cross)
    units = totals + [shape(rows, 128, jnp.float32)] * 2
    total1, total2, unit1, unit2, size1, size2 = call(
        own_kernel, totals + units, [SMEM] + [VMEM] * 12, [VMEM] * 6
    )(scalars, *blocks, raw11, raw12, raw21, raw22, norm11, norm12, norm21, norm22)
    total1, total2 = add(cross_kernel, total1, total2, cross1)
    near_a, far_a, total1, total2, both2 = lax.optimization_barrier(
        (near_a, far_a, total1, total2, both2)
    )
    far_next_a, near_next_a = send(near_a, far), send(far_a, near)
    cross2 = send(both2, cross)
    total1, total2 = add(add_kernel, total1, total2, near_a, far_a)
    near_b, far_b, total1, total2 = lax.optimization_barrier((near_b, far_b, total1, total2))
    far_next_b, near_next_b = send(near_b, far), send(far_b, near)
    total1, total2 = add(add_kernel, total1, total2, near_b, far_b)
    total1, total2 = add(add_kernel, total1, total2, near_next_a, far_next_a)
    total1, total2 = add(cross_kernel, total1, total2, cross2)

    def last(body, given, *operands):
        return call(
            body,
            [shape(rows, width, jnp.bfloat16)] * 2,
            [SMEM] * 2 + [VMEM] * 6 + [HBM] * given,
            [HBM] * 2,
            [pltpu.VMEM((rows, width), jnp.bfloat16), pltpu.SemaphoreType.DMA((rows // TILE,))],
            aliases={8: 0, 9: 1} if given else None,
        )(scalars, even, *operands)

    grads = last(first_last_kernel, 0, first1, first2, near_next_b, total1, unit1, size1)
    return last(
        functools.partial(last_kernel, 1), 2, second1, second2, far_next_b, total2, unit2, size2, *grads
    )


def solution(mesh):
    spec = P(AXES, None)
    return jax.shard_map(
        on_device,
        mesh=mesh,
        in_specs=(spec, spec, P(), P()),
        out_specs=(spec, spec),
        check_vma=False,
    )
```

```python
import functools

import jax
import jax.numpy as jnp
from jax import lax
from jax.experimental import pallas as pl
from jax.experimental.pallas import tpu as pltpu
from jax.sharding import PartitionSpec as P

AXES = ("grp", "blk")
VMEM = pl.BlockSpec(memory_space=pltpu.VMEM)
SMEM = pl.BlockSpec(memory_space=pltpu.SMEM)
HBM = pl.BlockSpec(memory_space=pltpu.HBM)
TILE = 128
MIB = 1024 * 1024


def routes(groups, blocks):
    near, far, cross = [], [], []
    for g in range(groups):
        for k in range(blocks):
            me = g * blocks + k
            near.append((me, g * blocks + (k ^ 1)))
            other = (k + 1) % blocks if k % 2 else (k - 1) % blocks
            far.append((me, g * blocks + other))
            cross.append((me, (g ^ 1) * blocks + k))
    return near, far, cross


def call(body, outs, in_specs, out_specs, scratch=(), aliases=None, limit=16):
    return pl.pallas_call(
        body,
        out_shape=outs,
        in_specs=in_specs,
        out_specs=out_specs,
        scratch_shapes=scratch,
        input_output_aliases=aliases or {},
        compiler_params=pltpu.CompilerParams(vmem_limit_bytes=limit * MIB),
        cost_estimate=pl.CostEstimate(flops=0, bytes_accessed=0, transcendentals=0),
    )


def shape(rows, width, dtype):
    return jax.ShapeDtypeStruct((rows, width), dtype)


def prepare_kernel(start, even, images, texts, *refs):
    *outs, both, sems = refs
    blocks = (outs[:3], outs[3:])
    rows = blocks[0][0].shape[0]
    tiles = rows // TILE

    def fetch(slot, source, tile):
        return pltpu.make_async_copy(
            source.at[pl.ds(start + tile * TILE, TILE)],
            blocks[slot][1].at[pl.ds(tile * TILE, TILE)],
            sems.at[slot, tile],
        )

    def begin(sources):
        for tile in range(tiles):
            for slot, source in enumerate(sources):
                fetch(slot, source, tile).start()

    @pl.when(even[0] == 1)
    def _():
        begin((texts, images))

    @pl.when(even[0] != 1)
    def _():
        begin((images, texts))

    for tile in range(tiles):
        at = pl.ds(tile * TILE, TILE)
        for slot, (half, raw, norm) in enumerate(blocks):
            fetch(slot, images, tile).wait()
            values = raw[at].astype(jnp.float32)
            inverse = lax.rsqrt(jnp.sum(values * values, axis=-1, keepdims=True) + 1e-06)
            rounded = (values * inverse).astype(jnp.bfloat16)
            half[at] = rounded
            both[pl.ds(slot * rows + tile * TILE, TILE)] = rounded
            norm[at] = jnp.broadcast_to(inverse, (TILE, 128))


def prepare(start, rows, even, images, texts):
    width = images.shape[1]
    rounded = shape(rows, width, jnp.bfloat16)
    outs = [rounded, rounded, shape(rows, 128, jnp.float32)] * 2
    outs.append(shape(2 * rows, width, jnp.bfloat16))
    return call(
        functools.partial(prepare_kernel, start),
        outs,
        [SMEM, HBM, HBM],
        [VMEM] * len(outs),
        [pltpu.SemaphoreType.DMA((2, rows // TILE))],
        limit=50,
    )(even, images, texts)


def coefficients(scale, bias, left, right, diagonal=False):
    dots = lax.dot_general(left, right, (((1,), (1,)), ((), ())), preferred_element_type=jnp.float32)
    power = dots * (-scale) - bias
    if not diagonal:
        return (scale / (1.0 + jnp.exp(power))).astype(jnp.bfloat16)
    here = lax.broadcasted_iota(jnp.int32, dots.shape, 0) == lax.broadcasted_iota(
        jnp.int32, dots.shape, 1
    )
    factor = jnp.where(here, -scale, scale)
    return (factor / (1.0 + jnp.exp(jnp.where(here, -power, power)))).astype(jnp.bfloat16)


def product(coef, right):
    return jnp.dot(coef, right, preferred_element_type=jnp.float32)


def own_kernel(
    scalars, first1, first2, second1, second2,
    raw11, raw12, raw21, raw22, norm11, norm12, norm21, norm22,
    total1, total2, unit1, unit2, size1, size2,
):
    scale, bias = scalars[0], scalars[1]
    firsts, seconds = (first1, first2), (second1, second2)
    rows = first1.shape[0]
    for lefts, rights, total in ((firsts, seconds, total1), (seconds, firsts, total2)):
        for i, left in enumerate(lefts):
            at = pl.ds(i * rows, rows)
            for j, right in enumerate(rights):
                term = product(coefficients(scale, bias, left[...], right[...], i == j), right[...])
                total[at] = term if j == 0 else total[at] + term
    for raws, norms, unit, size in (
        ((raw11, raw12), (norm11, norm12), unit1, size1),
        ((raw21, raw22), (norm21, norm22), unit2, size2),
    ):
        for i in range(2):
            at = pl.ds(i * rows, rows)
            unit[at] = raws[i][...].astype(jnp.float32) * norms[i][:, :1]
            size[at] = norms[i][...]


def add_kernel(scalars, first1, first2, second1, second2, in1, in2, right1, right2, total1, total2):
    scale, bias = scalars[0], scalars[1]
    rows = first1.shape[0]
    for lefts, right, given, total in (
        ((first1, first2), right1, in1, total1),
        ((second1, second2), right2, in2, total2),
    ):
        for i, left in enumerate(lefts):
            at = pl.ds(i * rows, rows)
            total[at] = given[at] + product(coefficients(scale, bias, left[...], right[...]), right[...])


def cross_kernel(scalars, first1, first2, second1, second2, in1, in2, both, total1, total2):
    rows = first1.shape[0]
    add_kernel(
        scalars, first1, first2, second1, second2, in1, in2,
        both.at[pl.ds(rows, rows)], both.at[pl.ds(0, rows)], total1, total2,
    )


def last_kernel(
    slot, scalars, even, left1, left2, right, given, unit, norm, image_in, text_in,
    image_grad, text_grad, out, sems,
):
    del image_in, text_in
    scale, bias = scalars[0], scalars[1]
    rows = left1.shape[0]

    def give(tile, target):
        at = pl.ds(tile * TILE, TILE)
        return pltpu.make_async_copy(out.at[at], target.at[at], sems.at[tile])

    coefs = [coefficients(scale, bias, left[...], right[...]) for left in (left1, left2)]
    tiles = 2 * rows // TILE
    for tile in range(tiles):
        i, inner = divmod(tile * TILE, rows)
        at = pl.ds(tile * TILE, TILE)
        whole = given[at] + product(coefs[i][inner : inner + TILE], right[...])
        along = jnp.sum(unit[at] * whole, axis=-1, keepdims=True)
        out[at] = ((whole - unit[at] * along) * norm[at][:, :1]).astype(jnp.bfloat16)

        @pl.when((even[0] == 1) == (slot == 0))
        def _():
            give(tile, text_grad).start()

        @pl.when((even[0] == 1) != (slot == 0))
        def _():
            give(tile, image_grad).start()

    for tile in range(tiles):
        give(tile, text_grad).wait()


def first_last_kernel(scalars, even, left1, left2, right, given, unit, norm, *refs):
    last_kernel(0, scalars, even, left1, left2, right, given, unit, norm, None, None, *refs)


def on_device(images, texts, logit_scale, logit_bias):
    rows, width = images.shape
    near, far, cross = routes(lax.axis_size("grp"), lax.axis_size("blk"))
    even = (1 - lax.axis_index("blk") % 2).astype(jnp.int32).reshape(1)
    scalars = jnp.concatenate([logit_scale, logit_bias])

    half = rows // 2
    first1, raw11, norm11, second1, raw21, norm21, both1 = prepare(
        0, half, even, images, texts
    )
    first2, raw12, norm12, second2, raw22, norm22, both2 = prepare(
        half, half, even, images, texts
    )

    def send(block, route):
        return lax.ppermute(block, AXES, route)

    blocks = (first1, first2, second1, second2)
    totals = [shape(rows, width, jnp.float32)] * 2

    def add(body, total1, total2, *rights):
        return call(
            body, totals, [SMEM] + [VMEM] * (6 + len(rights)), [VMEM] * 2, aliases={5: 0, 6: 1}
        )(scalars, *blocks, total1, total2, *rights)

    far_a, near_a = send(second1, far), send(first1, near)
    far_b, near_b = send(second2, far), send(first2, near)
    cross1 = send(both1, cross)
    units = totals + [shape(rows, 128, jnp.float32)] * 2
    total1, total2, unit1, unit2, size1, size2 = call(
        own_kernel, totals + units, [SMEM] + [VMEM] * 12, [VMEM] * 6
    )(scalars, *blocks, raw11, raw12, raw21, raw22, norm11, norm12, norm21, norm22)
    near_a, far_a, total1, total2, both2 = lax.optimization_barrier(
        (near_a, far_a, total1, total2, both2)
    )
    far_next_a, near_next_a = send(near_a, far), send(far_a, near)
    cross2 = send(both2, cross)
    total1, total2 = add(cross_kernel, total1, total2, cross1)
    total1, total2 = add(add_kernel, total1, total2, near_a, far_a)
    near_b, far_b, total1, total2 = lax.optimization_barrier((near_b, far_b, total1, total2))
    far_next_b, near_next_b = send(near_b, far), send(far_b, near)
    total1, total2 = add(add_kernel, total1, total2, near_b, far_b)
    total1, total2 = add(add_kernel, total1, total2, near_next_a, far_next_a)
    total1, total2 = add(cross_kernel, total1, total2, cross2)

    def last(body, given, *operands):
        return call(
            body,
            [shape(rows, width, jnp.bfloat16)] * 2,
            [SMEM] * 2 + [VMEM] * 6 + [HBM] * given,
            [HBM] * 2,
            [pltpu.VMEM((rows, width), jnp.bfloat16), pltpu.SemaphoreType.DMA((rows // TILE,))],
            aliases={8: 0, 9: 1} if given else None,
        )(scalars, even, *operands)

    grads = last(first_last_kernel, 0, first1, first2, near_next_b, total1, unit1, size1)
    return last(
        functools.partial(last_kernel, 1), 2, second1, second2, far_next_b, total2, unit2, size2, *grads
    )


def solution(mesh):
    spec = P(AXES, None)
    return jax.shard_map(
        on_device,
        mesh=mesh,
        in_specs=(spec, spec, P(), P()),
        out_specs=(spec, spec),
        check_vma=False,
    )
```

```python
import functools

import jax
import jax.numpy as jnp
from jax import lax
from jax.experimental import pallas as pl
from jax.experimental.pallas import tpu as pltpu
from jax.sharding import PartitionSpec as P

AXES = ("grp", "blk")
VMEM = pl.BlockSpec(memory_space=pltpu.VMEM)
SMEM = pl.BlockSpec(memory_space=pltpu.SMEM)
HBM = pl.BlockSpec(memory_space=pltpu.HBM)
TILE = 128
MIB = 1024 * 1024


def routes(groups, blocks):
    near, far, cross = [], [], []
    for g in range(groups):
        for k in range(blocks):
            me = g * blocks + k
            near.append((me, g * blocks + (k ^ 1)))
            other = (k + 1) % blocks if k % 2 else (k - 1) % blocks
            far.append((me, g * blocks + other))
            cross.append((me, (g ^ 1) * blocks + k))
    return near, far, cross


def call(body, outs, in_specs, out_specs, scratch=(), aliases=None, limit=16):
    return pl.pallas_call(
        body,
        out_shape=outs,
        in_specs=in_specs,
        out_specs=out_specs,
        scratch_shapes=scratch,
        input_output_aliases=aliases or {},
        compiler_params=pltpu.CompilerParams(vmem_limit_bytes=limit * MIB),
        cost_estimate=pl.CostEstimate(flops=0, bytes_accessed=0, transcendentals=0),
    )


def shape(rows, width, dtype):
    return jax.ShapeDtypeStruct((rows, width), dtype)


def prepare_kernel(start, even, images, texts, *refs):
    *outs, both, sems = refs
    blocks = (outs[:3], outs[3:])
    rows = blocks[0][0].shape[0]

    def fetch(slot, source):
        return pltpu.make_async_copy(
            source.at[pl.ds(start, rows)], blocks[slot][1], sems.at[slot]
        )

    @pl.when(even[0] == 1)
    def _():
        fetch(0, texts).start()
        fetch(1, images).start()

    @pl.when(even[0] != 1)
    def _():
        fetch(0, images).start()
        fetch(1, texts).start()

    for slot, (half, raw, norm) in enumerate(blocks):
        fetch(slot, images).wait()
        values = raw[...].astype(jnp.float32)
        inverse = lax.rsqrt(jnp.sum(values * values, axis=-1, keepdims=True) + 1e-06)
        rounded = (values * inverse).astype(jnp.bfloat16)
        half[...] = rounded
        both[pl.ds(slot * rows, rows)] = rounded
        norm[...] = jnp.broadcast_to(inverse, (rows, 128))


def prepare(start, rows, even, images, texts):
    width = images.shape[1]
    rounded = shape(rows, width, jnp.bfloat16)
    outs = [rounded, rounded, shape(rows, 128, jnp.float32)] * 2
    outs.append(shape(2 * rows, width, jnp.bfloat16))
    return call(
        functools.partial(prepare_kernel, start),
        outs,
        [SMEM, HBM, HBM],
        [VMEM] * len(outs),
        [pltpu.SemaphoreType.DMA((2,))],
        limit=50,
    )(even, images, texts)


def coefficients(scale, bias, left, right, diagonal=False):
    dots = lax.dot_general(left, right, (((1,), (1,)), ((), ())), preferred_element_type=jnp.float32)
    power = dots * (-scale) - bias
    if not diagonal:
        return (scale / (1.0 + jnp.exp(power))).astype(jnp.bfloat16)
    here = lax.broadcasted_iota(jnp.int32, dots.shape, 0) == lax.broadcasted_iota(
        jnp.int32, dots.shape, 1
    )
    factor = jnp.where(here, -scale, scale)
    return (factor / (1.0 + jnp.exp(jnp.where(here, -power, power)))).astype(jnp.bfloat16)


def product(coef, right):
    return jnp.dot(coef, right, preferred_element_type=jnp.float32)


def own_kernel(
    scalars, first1, first2, second1, second2,
    raw11, raw12, raw21, raw22, norm11, norm12, norm21, norm22,
    total1, total2, unit1, unit2, size1, size2,
):
    scale, bias = scalars[0], scalars[1]
    firsts, seconds = (first1, first2), (second1, second2)
    rows = first1.shape[0]
    for lefts, rights, total in ((firsts, seconds, total1), (seconds, firsts, total2)):
        for i, left in enumerate(lefts):
            at = pl.ds(i * rows, rows)
            for j, right in enumerate(rights):
                term = product(coefficients(scale, bias, left[...], right[...], i == j), right[...])
                total[at] = term if j == 0 else total[at] + term
    for raws, norms, unit, size in (
        ((raw11, raw12), (norm11, norm12), unit1, size1),
        ((raw21, raw22), (norm21, norm22), unit2, size2),
    ):
        for i in range(2):
            at = pl.ds(i * rows, rows)
            unit[at] = raws[i][...].astype(jnp.float32) * norms[i][:, :1]
            size[at] = norms[i][...]


def add_kernel(scalars, first1, first2, second1, second2, in1, in2, right1, right2, total1, total2):
    scale, bias = scalars[0], scalars[1]
    rows = first1.shape[0]
    for lefts, right, given, total in (
        ((first1, first2), right1, in1, total1),
        ((second1, second2), right2, in2, total2),
    ):
        for i, left in enumerate(lefts):
            at = pl.ds(i * rows, rows)
            total[at] = given[at] + product(coefficients(scale, bias, left[...], right[...]), right[...])


def cross_kernel(scalars, first1, first2, second1, second2, in1, in2, both, total1, total2):
    rows = first1.shape[0]
    add_kernel(
        scalars, first1, first2, second1, second2, in1, in2,
        both.at[pl.ds(rows, rows)], both.at[pl.ds(0, rows)], total1, total2,
    )


def last_kernel(
    slot, scalars, even, left1, left2, right, given, unit, norm, image_in, text_in,
    image_grad, text_grad, out, sems,
):
    del image_in, text_in
    scale, bias = scalars[0], scalars[1]
    rows = left1.shape[0]

    def give(tile, target):
        at = pl.ds(tile * TILE, TILE)
        return pltpu.make_async_copy(out.at[at], target.at[at], sems.at[tile])

    coefs = [coefficients(scale, bias, left[...], right[...]) for left in (left1, left2)]
    tiles = 2 * rows // TILE
    for tile in range(tiles):
        i, inner = divmod(tile * TILE, rows)
        at = pl.ds(tile * TILE, TILE)
        whole = given[at] + product(coefs[i][inner : inner + TILE], right[...])
        along = jnp.sum(unit[at] * whole, axis=-1, keepdims=True)
        out[at] = ((whole - unit[at] * along) * norm[at][:, :1]).astype(jnp.bfloat16)

        @pl.when((even[0] == 1) == (slot == 0))
        def _():
            give(tile, text_grad).start()

        @pl.when((even[0] == 1) != (slot == 0))
        def _():
            give(tile, image_grad).start()

    for tile in range(tiles):
        give(tile, text_grad).wait()


def first_last_kernel(scalars, even, left1, left2, right, given, unit, norm, *refs):
    last_kernel(0, scalars, even, left1, left2, right, given, unit, norm, None, None, *refs)


def on_device(images, texts, logit_scale, logit_bias):
    rows, width = images.shape
    near, far, cross = routes(lax.axis_size("grp"), lax.axis_size("blk"))
    even = (1 - lax.axis_index("blk") % 2).astype(jnp.int32).reshape(1)
    scalars = jnp.concatenate([logit_scale, logit_bias])

    half = rows // 2
    first1, raw11, norm11, second1, raw21, norm21, both1 = prepare(
        0, half, even, images, texts
    )
    first2, raw12, norm12, second2, raw22, norm22, both2 = prepare(
        half, half, even, images, texts
    )

    def send(block, route):
        return lax.ppermute(block, AXES, route)

    blocks = (first1, first2, second1, second2)
    totals = [shape(rows, width, jnp.float32)] * 2

    def add(body, total1, total2, *rights):
        return call(
            body, totals, [SMEM] + [VMEM] * (6 + len(rights)), [VMEM] * 2, aliases={5: 0, 6: 1}
        )(scalars, *blocks, total1, total2, *rights)

    far_a, near_a = send(second1, far), send(first1, near)
    far_b, near_b = send(second2, far), send(first2, near)
    cross1 = send(both1, cross)
    units = totals + [shape(rows, 128, jnp.float32)] * 2
    total1, total2, unit1, unit2, size1, size2 = call(
        own_kernel, totals + units, [SMEM] + [VMEM] * 12, [VMEM] * 6
    )(scalars, *blocks, raw11, raw12, raw21, raw22, norm11, norm12, norm21, norm22)
    near_a, far_a, total1, total2, both2 = lax.optimization_barrier(
        (near_a, far_a, total1, total2, both2)
    )
    far_next_a, near_next_a = send(near_a, far), send(far_a, near)
    cross2 = send(both2, cross)
    total1, total2 = add(cross_kernel, total1, total2, cross1)
    total1, total2 = add(add_kernel, total1, total2, near_a, far_a)
    near_b, far_b, total1, total2 = lax.optimization_barrier((near_b, far_b, total1, total2))
    far_next_b, near_next_b = send(near_b, far), send(far_b, near)
    total1, total2 = add(add_kernel, total1, total2, near_b, far_b)
    total1, total2 = add(add_kernel, total1, total2, near_next_a, far_next_a)
    total1, total2 = add(cross_kernel, total1, total2, cross2)

    def last(body, given, *operands):
        return call(
            body,
            [shape(rows, width, jnp.bfloat16)] * 2,
            [SMEM] * 2 + [VMEM] * 6 + [HBM] * given,
            [HBM] * 2,
            [pltpu.VMEM((rows, width), jnp.bfloat16), pltpu.SemaphoreType.DMA((rows // TILE,))],
            aliases={8: 0, 9: 1} if given else None,
        )(scalars, even, *operands)

    grads = last(first_last_kernel, 0, first1, first2, near_next_b, total1, unit1, size1)
    return last(
        functools.partial(last_kernel, 1), 2, second1, second2, far_next_b, total2, unit2, size2, *grads
    )


def solution(mesh):
    spec = P(AXES, None)
    return jax.shard_map(
        on_device,
        mesh=mesh,
        in_specs=(spec, spec, P(), P()),
        out_specs=(spec, spec),
        check_vma=False,
    )
```

```python
import functools

import jax
import jax.numpy as jnp
from jax import lax
from jax.experimental import pallas as pl
from jax.experimental.pallas import tpu as pltpu
from jax.sharding import PartitionSpec as P

AXES = ("grp", "blk")
VMEM = pl.BlockSpec(memory_space=pltpu.VMEM)
SMEM = pl.BlockSpec(memory_space=pltpu.SMEM)
HBM = pl.BlockSpec(memory_space=pltpu.HBM)
TILE = 128
MIB = 1024 * 1024


def routes(groups, blocks):
    near, far, cross = [], [], []
    for g in range(groups):
        for k in range(blocks):
            me = g * blocks + k
            near.append((me, g * blocks + (k ^ 1)))
            other = (k + 1) % blocks if k % 2 else (k - 1) % blocks
            far.append((me, g * blocks + other))
            cross.append((me, (g ^ 1) * blocks + k))
    return near, far, cross


def call(body, outs, in_specs, out_specs, scratch=(), aliases=None, limit=16):
    return pl.pallas_call(
        body,
        out_shape=outs,
        in_specs=in_specs,
        out_specs=out_specs,
        scratch_shapes=scratch,
        input_output_aliases=aliases or {},
        compiler_params=pltpu.CompilerParams(vmem_limit_bytes=limit * MIB),
        cost_estimate=pl.CostEstimate(flops=0, bytes_accessed=0, transcendentals=0),
    )


def shape(rows, width, dtype):
    return jax.ShapeDtypeStruct((rows, width), dtype)


def prepare_kernel(start, even, images, texts, *refs):
    *outs, both, sems = refs
    blocks = (outs[:3], outs[3:])
    rows = blocks[0][0].shape[0]

    def fetch(slot, source):
        return pltpu.make_async_copy(
            source.at[pl.ds(start, rows)], blocks[slot][1], sems.at[slot]
        )

    @pl.when(even[0] == 1)
    def _():
        fetch(0, texts).start()
        fetch(1, images).start()

    @pl.when(even[0] != 1)
    def _():
        fetch(0, images).start()
        fetch(1, texts).start()

    for slot, (half, raw, norm) in enumerate(blocks):
        fetch(slot, images).wait()
        values = raw[...].astype(jnp.float32)
        inverse = lax.rsqrt(jnp.sum(values * values, axis=-1, keepdims=True) + 1e-06)
        rounded = (values * inverse).astype(jnp.bfloat16)
        half[...] = rounded
        both[pl.ds(slot * rows, rows)] = rounded
        norm[...] = jnp.broadcast_to(inverse, (rows, 128))


def prepare(start, rows, even, images, texts):
    width = images.shape[1]
    rounded = shape(rows, width, jnp.bfloat16)
    outs = [rounded, rounded, shape(rows, 128, jnp.float32)] * 2
    outs.append(shape(2 * rows, width, jnp.bfloat16))
    return call(
        functools.partial(prepare_kernel, start),
        outs,
        [SMEM, HBM, HBM],
        [VMEM] * len(outs),
        [pltpu.SemaphoreType.DMA((2,))],
        limit=50,
    )(even, images, texts)


def coefficients(scale, bias, left, right, diagonal=False):
    dots = lax.dot_general(left, right, (((1,), (1,)), ((), ())), preferred_element_type=jnp.float32)
    power = dots * (-scale) - bias
    if not diagonal:
        return (scale / (1.0 + jnp.exp(power))).astype(jnp.bfloat16)
    here = lax.broadcasted_iota(jnp.int32, dots.shape, 0) == lax.broadcasted_iota(
        jnp.int32, dots.shape, 1
    )
    factor = jnp.where(here, -scale, scale)
    return (factor / (1.0 + jnp.exp(jnp.where(here, -power, power)))).astype(jnp.bfloat16)


def product(coef, right):
    return jnp.dot(coef, right, preferred_element_type=jnp.float32)


def own_kernel(
    scalars, first1, first2, second1, second2,
    raw11, raw12, raw21, raw22, norm11, norm12, norm21, norm22,
    total1, total2, unit1, unit2, size1, size2,
):
    scale, bias = scalars[0], scalars[1]
    firsts, seconds = (first1, first2), (second1, second2)
    rows = first1.shape[0]
    for lefts, rights, total in ((firsts, seconds, total1), (seconds, firsts, total2)):
        for i, left in enumerate(lefts):
            at = pl.ds(i * rows, rows)
            for j, right in enumerate(rights):
                term = product(coefficients(scale, bias, left[...], right[...], i == j), right[...])
                total[at] = term if j == 0 else total[at] + term
    for raws, norms, unit, size in (
        ((raw11, raw12), (norm11, norm12), unit1, size1),
        ((raw21, raw22), (norm21, norm22), unit2, size2),
    ):
        for i in range(2):
            at = pl.ds(i * rows, rows)
            unit[at] = raws[i][...].astype(jnp.float32) * norms[i][:, :1]
            size[at] = norms[i][...]


def add_kernel(scalars, first1, first2, second1, second2, in1, in2, right1, right2, total1, total2):
    scale, bias = scalars[0], scalars[1]
    rows = first1.shape[0]
    for lefts, right, given, total in (
        ((first1, first2), right1, in1, total1),
        ((second1, second2), right2, in2, total2),
    ):
        for i, left in enumerate(lefts):
            at = pl.ds(i * rows, rows)
            total[at] = given[at] + product(coefficients(scale, bias, left[...], right[...]), right[...])


def cross_kernel(scalars, first1, first2, second1, second2, in1, in2, both, total1, total2):
    rows = first1.shape[0]
    add_kernel(
        scalars, first1, first2, second1, second2, in1, in2,
        both.at[pl.ds(rows, rows)], both.at[pl.ds(0, rows)], total1, total2,
    )


def last_kernel(
    slot, scalars, even, left1, left2, right, given, unit, norm, image_in, text_in,
    image_grad, text_grad, out, sems,
):
    del image_in, text_in
    scale, bias = scalars[0], scalars[1]
    rows = left1.shape[0]

    def give(tile, target):
        at = pl.ds(tile * TILE, TILE)
        return pltpu.make_async_copy(out.at[at], target.at[at], sems.at[tile])

    coefs = [coefficients(scale, bias, left[...], right[...]) for left in (left1, left2)]
    tiles = 2 * rows // TILE

    def term(tile):
        i, inner = divmod(tile * TILE, rows)
        return product(coefs[i][inner : inner + TILE], right[...])

    ahead = term(0)
    for tile in range(tiles):
        at = pl.ds(tile * TILE, TILE)
        whole = given[at] + ahead
        if tile < tiles - 1:
            ahead = term(tile + 1)
        along = jnp.sum(unit[at] * whole, axis=-1, keepdims=True)
        out[at] = ((whole - unit[at] * along) * norm[at][:, :1]).astype(jnp.bfloat16)

        @pl.when((even[0] == 1) == (slot == 0))
        def _():
            give(tile, text_grad).start()

        @pl.when((even[0] == 1) != (slot == 0))
        def _():
            give(tile, image_grad).start()

    for tile in range(tiles):
        give(tile, text_grad).wait()


def first_last_kernel(scalars, even, left1, left2, right, given, unit, norm, *refs):
    last_kernel(0, scalars, even, left1, left2, right, given, unit, norm, None, None, *refs)


def on_device(images, texts, logit_scale, logit_bias):
    rows, width = images.shape
    near, far, cross = routes(lax.axis_size("grp"), lax.axis_size("blk"))
    even = (1 - lax.axis_index("blk") % 2).astype(jnp.int32).reshape(1)
    scalars = jnp.concatenate([logit_scale, logit_bias])

    half = rows // 2
    first1, raw11, norm11, second1, raw21, norm21, both1 = prepare(
        0, half, even, images, texts
    )
    first2, raw12, norm12, second2, raw22, norm22, both2 = prepare(
        half, half, even, images, texts
    )

    def send(block, route):
        return lax.ppermute(block, AXES, route)

    blocks = (first1, first2, second1, second2)
    totals = [shape(rows, width, jnp.float32)] * 2

    def add(body, total1, total2, *rights):
        return call(
            body, totals, [SMEM] + [VMEM] * (6 + len(rights)), [VMEM] * 2, aliases={5: 0, 6: 1}
        )(scalars, *blocks, total1, total2, *rights)

    far_a, near_a = send(second1, far), send(first1, near)
    far_b, near_b = send(second2, far), send(first2, near)
    cross1 = send(both1, cross)
    units = totals + [shape(rows, 128, jnp.float32)] * 2
    total1, total2, unit1, unit2, size1, size2 = call(
        own_kernel, totals + units, [SMEM] + [VMEM] * 12, [VMEM] * 6
    )(scalars, *blocks, raw11, raw12, raw21, raw22, norm11, norm12, norm21, norm22)
    near_a, far_a, total1, total2, both2 = lax.optimization_barrier(
        (near_a, far_a, total1, total2, both2)
    )
    far_next_a, near_next_a = send(near_a, far), send(far_a, near)
    cross2 = send(both2, cross)
    total1, total2 = add(cross_kernel, total1, total2, cross1)
    total1, total2 = add(add_kernel, total1, total2, near_a, far_a)
    near_b, far_b, total1, total2 = lax.optimization_barrier((near_b, far_b, total1, total2))
    far_next_b, near_next_b = send(near_b, far), send(far_b, near)
    total1, total2 = add(add_kernel, total1, total2, near_b, far_b)
    total1, total2 = add(add_kernel, total1, total2, near_next_a, far_next_a)
    total1, total2 = add(cross_kernel, total1, total2, cross2)

    def last(body, given, *operands):
        return call(
            body,
            [shape(rows, width, jnp.bfloat16)] * 2,
            [SMEM] * 2 + [VMEM] * 6 + [HBM] * given,
            [HBM] * 2,
            [pltpu.VMEM((rows, width), jnp.bfloat16), pltpu.SemaphoreType.DMA((rows // TILE,))],
            aliases={8: 0, 9: 1} if given else None,
        )(scalars, even, *operands)

    grads = last(first_last_kernel, 0, first1, first2, near_next_b, total1, unit1, size1)
    return last(
        functools.partial(last_kernel, 1), 2, second1, second2, far_next_b, total2, unit2, size2, *grads
    )


def solution(mesh):
    spec = P(AXES, None)
    return jax.shard_map(
        on_device,
        mesh=mesh,
        in_specs=(spec, spec, P(), P()),
        out_specs=(spec, spec),
        check_vma=False,
    )
```
